256 devices in a mesh: seq: 32 (over x, y, core), uly: 8 (over z).
Axes of the slice: x: 4, y: 4, z: 8, core: 2. Of those that a mesh axis runs over, the one named last changes fastest.
Arguments:
- queries: bfloat16 [32768, 5120], P(('seq', 'uly')), may hold values from -12 to 12
- keys: bfloat16 [32768, 5120], P(('seq', 'uly')), may hold values from -12 to 12
- values: bfloat16 [32768, 5120], P(('seq', 'uly')), may hold values from -6 to 6
- out_grad: bfloat16 [32768, 5120], P(('seq', 'uly')), may hold values from -6 to 6
- tile_offset: int32 [256], replicated, may hold values from 0 to 3, as said below
Outputs:
- attended: bfloat16 [32768, 5120], P(('seq', 'uly'))
- query_grad: bfloat16 [32768, 5120], P(('seq', 'uly'))
- key_grad: bfloat16 [32768, 5120], P(('seq', 'uly'))
- value_grad: bfloat16 [32768, 5120], P(('seq', 'uly'))
The draws below stay inside these ranges and needn't reach their ends.
Inputs may be any that keep to these rules, and one draw needn't show every extreme that they name: Clips are packed in order, each of whole tiles of 128 rows, and tile_offset[t] counts the tiles of t's clip before tile t. A clip begins at tile 0 and at every tile t with t % 4 == 2, and at no other tile t > 0 with t % (8) == 0. No clip has more than 4 tiles and some clip has exactly 4.
All inputs are finite; a program needn't handle non-finite values.
Results may differ from the reference program's by a relative error of at most 0.02.
Values may be sent and summed in bfloat16 or wider, within the bound.
No kernel may reach another device: no remote copies, remote signals or barrier semaphores. Data moves between devices by JAX's collectives and lax.ppermute only.
A program may use at most 128 MiB of HBM per device.

```python
import math
import jax
import jax.numpy as jnp
from jax import lax

H = 40
HD = 128
TILE = 128
DW = 5120
TOKENS = 32768
TILES = 256
MOST = 4


def scaled_rows(key, spread_low, spread_high):
    return jnp.exp(jax.random.uniform(key, (TOKENS, 1), jnp.float32, math.log(spread_low), math.log(spread_high)))


def draw_queries(key, part):
    own_key = jax.random.fold_in(key, 21)
    total_width = H * HD
    drawn_draw = jnp.clip(jax.random.normal(jax.random.fold_in(own_key, 2), (TOKENS, total_width), jnp.float32), -4.0, 4.0)
    result = drawn_draw * scaled_rows(jax.random.fold_in(own_key, 1), 0.3, 3.0)
    return result.astype(jnp.bfloat16)


def draw_keys(key, part):
    own_key = jax.random.fold_in(key, 22)
    total_width = H * HD
    drawn_draw = jnp.clip(jax.random.normal(jax.random.fold_in(own_key, 2), (TOKENS, total_width), jnp.float32), -4.0, 4.0)
    result = drawn_draw * scaled_rows(jax.random.fold_in(own_key, 1), 0.3, 3.0)
    return result.astype(jnp.bfloat16)


def draw_tile_offset(key, part):
    key = jax.random.fold_in(key, 23)
    index = jnp.arange(TILES, dtype=jnp.int32)
    forced = (index == 0) | (index % MOST == MOST // 2)
    barred = (index % (2 * MOST) == 0) & (index > 0)
    coins = jax.random.randint(jax.random.fold_in(key, 1), (TILES,), 0, 2)
    chosen = jax.random.randint(jax.random.fold_in(key, 2), (), 0, TILES // MOST - 1)
    opening = MOST // 2 + chosen * MOST
    inside = (index > opening) & (index < opening + MOST)
    starts = forced | (coins == 1) & jnp.logical_not(barred) & jnp.logical_not(inside)
    latest = lax.cummax(jnp.where(starts, index, 0), axis=0)
    return (index - latest).astype(jnp.int32)


def level_of(key, shape, shards, least, top_value):
    def one(position, blocks):
        steps = jax.random.uniform(jax.random.fold_in(jax.random.fold_in(key, 6), position), (blocks,), jnp.float32, least / len(shards), top_value / len(shards))
        return jnp.repeat(jnp.exp(steps), shape[position] // blocks).reshape((-1,) + (1,) * (len(shape) - position - 1))

    loudness = one(*shards[0])
    for cut in shards[1:]:
        loudness = loudness * one(*cut)
    return loudness


def centred(key, dims, width, bound, split=(), kind=jnp.bfloat16):
    values = jax.random.normal(key, dims, jnp.float32) * width
    if len(split) > 0:
        values = level_of(key, dims, split, -0.22, 0.18) * values
    return jnp.clip(values, min=-bound, max=bound).astype(kind)


def setup_inputs(seed: int = 0) -> dict:
    key_of = jax.random.split(jax.random.key(seed), 6)
    queries = draw_queries(jax.random.fold_in(key_of[5], 71), 0)
    keys = draw_keys(jax.random.fold_in(key_of[5], 71), 0)
    values = centred(key_of[2], (TOKENS, DW), 1.0, 6.0, ((0, 256),))
    out_grad = centred(key_of[3], (TOKENS, DW), 1.0, 6.0, ((0, 256),))
    tile_offset = draw_tile_offset(jax.random.fold_in(key_of[5], 71), 0)
    return dict(queries=queries, keys=keys, values=values, out_grad=out_grad, tile_offset=tile_offset)


def clip_firsts(tile_offset):
    tile_count = tile_offset.shape[0]
    firsts = jnp.arange(tile_count, dtype=jnp.int32) - tile_offset
    return jnp.broadcast_to(firsts[:, None], (tile_count, TILE)).reshape(-1)


def head_pass(head_index, queries, keys, values, out_grad, row_first):
    reach_rows = MOST * TILE
    factor = HD ** -0.5

    def columns(source):
        return lax.dynamic_slice_in_dim(source, head_index * HD, HD, 1)

    query_head = columns(queries)
    grad_head = columns(out_grad)
    border = jnp.zeros((reach_rows, HD), jnp.bfloat16)
    key_pad = jnp.concatenate((border, columns(keys), border), axis=0)
    value_pad = jnp.concatenate((border, columns(values), border), axis=0)
    outside = jnp.full((reach_rows,), -1, jnp.int32)
    first_pad = jnp.concatenate((outside, row_first, outside))
    blocks = TOKENS // reach_rows

    def block_step(totals, block_index):
        key_total, value_total = totals
        row_begin = block_index * reach_rows
        query_rows = lax.dynamic_slice_in_dim(query_head, row_begin, reach_rows, 0)
        grad_rows = lax.dynamic_slice_in_dim(grad_head, row_begin, reach_rows, 0)
        key_window = lax.dynamic_slice_in_dim(key_pad, row_begin, 3 * reach_rows, 0)
        value_window = lax.dynamic_slice_in_dim(value_pad, row_begin, 3 * reach_rows, 0)
        query_first = lax.dynamic_slice_in_dim(row_first, row_begin, reach_rows, 0)
        key_first = lax.dynamic_slice_in_dim(first_pad, row_begin, 3 * reach_rows, 0)
        raw_scores = jnp.dot(query_rows, key_window.T, preferred_element_type=jnp.float32) * factor
        scores = jnp.where(query_first[:, None] == key_first[None, :], raw_scores, -jnp.inf)
        row_max = jnp.max(scores, axis=1)
        log_total = row_max + jnp.log(jnp.sum(jnp.exp(scores - row_max[:, None]), axis=1))
        weights = jnp.exp(scores - log_total[:, None])
        weights_half = weights.astype(jnp.bfloat16)
        attended = jnp.dot(weights_half, value_window, preferred_element_type=jnp.float32).astype(jnp.bfloat16)
        row_delta = jnp.sum(grad_rows.astype(jnp.float32) * attended.astype(jnp.float32), axis=1)
        dweights = jnp.dot(grad_rows, value_window.T, preferred_element_type=jnp.float32)
        dscores = (weights * (dweights - row_delta[:, None])).astype(jnp.bfloat16)
        query_part = (jnp.dot(dscores, key_window, preferred_element_type=jnp.float32) * factor).astype(jnp.bfloat16)
        key_part = jnp.dot(dscores.T, query_rows, preferred_element_type=jnp.float32) * factor
        value_part = jnp.dot(weights_half.T, grad_rows, preferred_element_type=jnp.float32)
        key_now = lax.dynamic_slice_in_dim(key_total, row_begin, 3 * reach_rows, 0)
        value_now = lax.dynamic_slice_in_dim(value_total, row_begin, 3 * reach_rows, 0)
        key_total = lax.dynamic_update_slice_in_dim(key_total, key_now + key_part, row_begin, 0)
        value_total = lax.dynamic_update_slice_in_dim(value_total, value_now + value_part, row_begin, 0)
        return (key_total, value_total), (attended, query_part)

    zero_total = jnp.zeros((TOKENS + 2 * reach_rows, HD), jnp.float32)
    totals, pieces = lax.scan(block_step, (zero_total, zero_total), jnp.arange(blocks, dtype=jnp.int32))
    key_total, value_total = totals
    attended = pieces[0].reshape(TOKENS, HD)
    query_grad = pieces[1].reshape(TOKENS, HD)
    key_grad = key_total[reach_rows:reach_rows + TOKENS].astype(jnp.bfloat16)
    value_grad = value_total[reach_rows:reach_rows + TOKENS].astype(jnp.bfloat16)
    return attended, query_grad, key_grad, value_grad


def reference(queries, keys, values, out_grad, tile_offset):
    row_first = clip_firsts(tile_offset)

    def single_head(head_index):
        return head_pass(head_index, queries, keys, values, out_grad, row_first)

    results = lax.map(single_head, jnp.arange(H, dtype=jnp.int32))

    def to_rows(stacked):
        return jnp.transpose(stacked, (1, 0, 2)).reshape(TOKENS, H * HD)

    return (to_rows(results[0]), to_rows(results[1]), to_rows(results[2]), to_rows(results[3]))
```

```python
from functools import partial

import jax
import jax.numpy as jnp
from jax import lax
from jax.experimental import pallas as pl
from jax.experimental.pallas import tpu as pltpu
from jax.sharding import PartitionSpec as P

HD = 128
TILE = 128
MOST = 4
AXES = ("seq", "uly")
CHUNKS = (2, 2, 2, 2, 2)
ORDER = (1, 2, 3)


def turns(step, tiles):
    def tile_at(window, place):
        return (MOST * window + place - MOST // 2) % tiles

    return [
        (tile_at(window, place), tile_at(window, (place + step) % MOST))
        for window in range(tiles // MOST)
        for place in range(MOST)
    ]


def place_at(step):
    return (lax.axis_index("uly") + MOST // 2 + step) % MOST


def pack_kernel(begin, heads_each, width, q_ref, k_ref, v_ref, g_ref, *rest):
    outs, sems = rest[-4:-1], rest[-1]
    copies = []
    for step in range(1, MOST):
        column = pl.multiple_of((place_at(step) * heads_each + begin) * HD, HD)
        for member, source in enumerate((q_ref, k_ref, v_ref, g_ref)):
            copies.append(
                pltpu.make_async_copy(
                    source.at[:, pl.ds(column, width)],
                    outs[step - 1].at[member],
                    sems.at[step - 1, member],
                )
            )
    for copy in copies:
        copy.start()
    for copy in copies:
        copy.wait()


def pack(arrays, after, begin, heads, heads_each):
    width = heads * HD
    piece = jax.ShapeDtypeStruct((4, TILE, width), jnp.bfloat16)
    return pl.pallas_call(
        partial(pack_kernel, begin, heads_each, width),
        out_shape=(piece,) * 3,
        in_specs=[pl.BlockSpec(memory_space=pl.ANY)] * (4 + len(after)),
        out_specs=(pl.BlockSpec(memory_space=pltpu.VMEM),) * 3,
        scratch_shapes=[pltpu.SemaphoreType.DMA((3, 4))],
        cost_estimate=pl.CostEstimate(flops=0, bytes_accessed=24 * TILE * width * 2, transcendentals=0),
        name="pack",
    )(*arrays, *after)


def unpack_kernel(begin, heads_each, width, *rest):
    pieces = rest[:4]
    outs, sems = rest[-5:-1], rest[-1]
    copies = []
    for step in range(MOST):
        column = pl.multiple_of((place_at(step) * heads_each + begin) * HD, HD)
        for member, target in enumerate(outs):
            copies.append(
                pltpu.make_async_copy(
                    pieces[step].at[member],
                    target.at[:, pl.ds(column, width)],
                    sems.at[step, member],
                )
            )
    for copy in copies:
        copy.start()
    for copy in copies:
        copy.wait()


def unpack(pieces, held, begin, heads, heads_each, columns):
    width = heads * HD
    whole = jax.ShapeDtypeStruct((TILE, columns), jnp.bfloat16)
    held = () if held is None else tuple(held)
    return pl.pallas_call(
        partial(unpack_kernel, begin, heads_each, width),
        out_shape=(whole,) * 4,
        in_specs=[pl.BlockSpec(memory_space=pltpu.VMEM)] * 4
        + [pl.BlockSpec(memory_space=pl.ANY)] * len(held),
        out_specs=(pl.BlockSpec(memory_space=pl.ANY),) * 4,
        scratch_shapes=[pltpu.SemaphoreType.DMA((4, 4))],
        input_output_aliases={4 + i: i for i in range(len(held))},
        cost_estimate=pl.CostEstimate(flops=0, bytes_accessed=32 * TILE * width * 2, transcendentals=0),
        name="unpack",
    )(*pieces, *held)


def matmul(left, right, left_dim, right_dim):
    return lax.dot_general(
        left, right, (((left_dim,), (right_dim,)), ((), ())), preferred_element_type=jnp.float32
    )


def attend_kernel(info, q_ref, k_ref, v_ref, g_ref, one, two, three, *rest):
    outs = rest[-4:]
    factor = HD ** -0.5
    rows = MOST * TILE

    def gather(own, member):
        return jnp.concatenate((own[...], one[member], two[member], three[member]), axis=0)

    q, k, v, g = (gather(own, i) for i, own in enumerate((q_ref, k_ref, v_ref, g_ref)))
    place = lax.broadcasted_iota(jnp.int32, (1, rows), 1) // TILE
    key_first = jnp.where(
        place < 2,
        jnp.where(place == 0, info[1], info[2]),
        jnp.where(place == 2, info[3], info[4]),
    )
    weights_all = []
    dscores_all = []
    for tile in range(MOST):
        part = slice(tile * TILE, (tile + 1) * TILE)
        query_rows, grad_rows = q[part], g[part]
        scores = matmul(query_rows, k, 1, 1) * factor
        scores = jnp.where(key_first == info[1 + tile], scores, -jnp.inf)
        row_max = jnp.max(scores, axis=1, keepdims=True)
        raised = jnp.exp(scores - row_max)
        weights = raised * (1.0 / jnp.sum(raised, axis=1, keepdims=True))
        half = weights.astype(jnp.bfloat16)
        attended = matmul(half, v, 1, 0).astype(jnp.bfloat16)
        delta = jnp.sum(
            grad_rows.astype(jnp.float32) * attended.astype(jnp.float32), axis=1, keepdims=True
        )
        dweights = matmul(grad_rows, v, 1, 1)
        dscores = (weights * (dweights - delta)).astype(jnp.bfloat16)
        outs[tile][0] = attended
        outs[tile][1] = (matmul(dscores, k, 1, 0) * factor).astype(jnp.bfloat16)
        weights_all.append(half)
        dscores_all.append(dscores)
    key_grad = (matmul(jnp.concatenate(dscores_all, axis=0), q, 0, 0) * factor).astype(jnp.bfloat16)
    value_grad = matmul(jnp.concatenate(weights_all, axis=0), g, 0, 0).astype(jnp.bfloat16)
    for tile in range(MOST):
        part = slice(tile * TILE, (tile + 1) * TILE)
        outs[tile][2] = key_grad[part]
        outs[tile][3] = value_grad[part]


def attend(info, arrays, received, after, begin, heads, heads_each):
    width = heads * HD
    piece = jax.ShapeDtypeStruct((4, TILE, width), jnp.bfloat16)
    own_spec = pl.BlockSpec((TILE, HD), lambda h, info: (0, info[0] * heads_each + begin + h))
    piece_spec = pl.BlockSpec((4, TILE, HD), lambda h, info: (0, 0, h))
    rows = MOST * TILE
    return pl.pallas_call(
        attend_kernel,
        out_shape=(piece,) * 4,
        grid_spec=pltpu.PrefetchScalarGridSpec(
            num_scalar_prefetch=1,
            grid=(heads,),
            in_specs=[own_spec] * 4
            + [piece_spec] * 3
            + [pl.BlockSpec(memory_space=pl.ANY)] * len(after),
            out_specs=(piece_spec,) * 4,
        ),
        cost_estimate=pl.CostEstimate(
            flops=12 * rows * rows * HD * heads,
            bytes_accessed=16 * rows * HD * heads,
            transcendentals=rows * rows * heads,
        ),
        name="attend",
    )(info, *arrays, *received, *after)


def shards(queries, keys, values, out_grad, tile_offset):
    arrays = (queries, keys, values, out_grad)
    columns = queries.shape[1]
    heads_each = columns // HD // MOST
    tiles = tile_offset.shape[0]
    device = lax.axis_index(AXES)
    place = (device + MOST // 2) % MOST
    places = (place - jnp.arange(MOST)) % MOST
    members = (device - place + places + tiles) % tiles
    firsts = members - tile_offset[members]
    info = jnp.concatenate((place[None], firsts)).astype(jnp.int32)

    def exchange(pieces, sign):
        done = {}
        for step in ORDER:
            done[step] = lax.ppermute(pieces[step - 1], AXES, turns(sign * step, tiles))
        return tuple(done[step] for step in (1, 2, 3))

    begins = [sum(CHUNKS[:i]) for i in range(len(CHUNKS))]
    received, after = [], ()
    for begin, heads in zip(begins, CHUNKS):
        pieces = pack(arrays, after, begin, heads, heads_each)
        after = pieces[:1]
        received.append(exchange(pieces, 1))
    results, after = [], ()
    for begin, heads, pieces in zip(begins, CHUNKS, received):
        own, *others = attend(info, arrays, pieces, after, begin, heads, heads_each)
        after = (own,)
        results.append((own, exchange(others, -1)))
    held = None
    for begin, heads, (own, others) in zip(begins, CHUNKS, results):
        held = unpack((own, *others), held, begin, heads, heads_each, columns)
    return tuple(held)


def solution(mesh):
    spec = P(AXES, None)
    return jax.shard_map(
        shards,
        mesh=mesh,
        in_specs=(spec, spec, spec, spec, P()),
        out_specs=(spec, spec, spec, spec),
        check_vma=False,
    )
```

```python
from functools import partial

import jax
import jax.numpy as jnp
from jax import lax
from jax.experimental import pallas as pl
from jax.experimental.pallas import tpu as pltpu
from jax.sharding import PartitionSpec as P

HD = 128
TILE = 128
MOST = 4
AXES = ("seq", "uly")
CHUNKS = (2, 2, 2, 2, 2)
TURNING = (True, False, False, False, False)
LAST = [(0, 1), (2,), (3,)]


def partner(place, step, turning):
    return (place + step) % MOST if turning else place ^ step


def routes(step, tiles, turning):
    def tile_at(window, place):
        return (MOST * window + place - MOST // 2) % tiles

    return [
        (tile_at(window, place), tile_at(window, partner(place, step, turning)))
        for window in range(tiles // MOST)
        for place in range(MOST)
    ]


def head_columns(step, turning, begin, heads_each, width):
    place = (lax.axis_index("uly") + MOST // 2) % MOST
    return pl.ds(pl.multiple_of((partner(place, step, turning) * heads_each + begin) * HD, HD), width)


def small_grant():
    return pltpu.CompilerParams(vmem_limit_bytes=16 * 1024 * 1024)


def pack_kernel(turning, begin, heads_each, width, q_ref, k_ref, v_ref, g_ref, *rest):
    outs, sems = rest[-4:-1], rest[-1]
    copies = []
    for step in range(1, MOST):
        columns = head_columns(step, turning, begin, heads_each, width)
        for member, source in enumerate((q_ref, k_ref, v_ref, g_ref)):
            copies.append(
                pltpu.make_async_copy(
                    source.at[:, columns],
                    outs[step - 1].at[member],
                    sems.at[step - 1, member],
                )
            )
    for copy in copies:
        copy.start()
    for copy in copies:
        copy.wait()


def pack(turning, arrays, after, begin, heads, heads_each):
    width = heads * HD
    piece = pltpu.VMEM((4, TILE, width), jnp.bfloat16)
    arrays = [pltpu.with_memory_space_constraint(array, pltpu.HBM) for array in arrays]
    return pl.pallas_call(
        partial(pack_kernel, turning, begin, heads_each, width),
        out_shape=(piece,) * 3,
        in_specs=[pl.BlockSpec(memory_space=pl.ANY)] * (4 + len(after)),
        out_specs=(pl.BlockSpec(memory_space=pltpu.VMEM),) * 3,
        scratch_shapes=[pltpu.SemaphoreType.DMA((3, 4))],
        compiler_params=small_grant(),
        cost_estimate=pl.CostEstimate(flops=0, bytes_accessed=24 * TILE * width * 2, transcendentals=0),
        name="pack",
    )(*arrays, *after)


def unpack_kernel(turning, steps, begin, heads_each, width, *rest):
    pieces = rest[: len(steps)]
    outs, sems = rest[-5:-1], rest[-1]
    copies = []
    for index, step in enumerate(steps):
        columns = head_columns(step, turning, begin, heads_each, width)
        for member, target in enumerate(outs):
            copies.append(
                pltpu.make_async_copy(
                    pieces[index].at[member],
                    target.at[:, columns],
                    sems.at[index, member],
                )
            )
    for copy in copies:
        copy.start()
    for copy in copies:
        copy.wait()


def unpack(turning, steps, pieces, held, begin, heads, heads_each, columns):
    width = heads * HD
    whole = jax.ShapeDtypeStruct((TILE, columns), jnp.bfloat16)
    return pl.pallas_call(
        partial(unpack_kernel, turning, steps, begin, heads_each, width),
        out_shape=(whole,) * 4,
        in_specs=[pl.BlockSpec(memory_space=pltpu.VMEM)] * len(steps)
        + [pl.BlockSpec(memory_space=pl.ANY)] * len(held),
        out_specs=(pl.BlockSpec(memory_space=pl.ANY),) * 4,
        scratch_shapes=[pltpu.SemaphoreType.DMA((len(steps), 4))],
        compiler_params=small_grant(),
        input_output_aliases={len(steps) + i: i for i in range(len(held))},
        cost_estimate=pl.CostEstimate(flops=0, bytes_accessed=8 * len(steps) * TILE * width * 2, transcendentals=0),
        name="unpack",
    )(*pieces, *held)


def matmul(left, right, left_dim, right_dim):
    return lax.dot_general(
        left, right, (((left_dim,), (right_dim,)), ((), ())), preferred_element_type=jnp.float32
    )


def attend_kernel(info, q_ref, k_ref, v_ref, g_ref, one, two, three, *rest):
    outs = rest[-4:]
    factor = HD ** -0.5
    rows = MOST * TILE

    def gather(own, member):
        return jnp.concatenate((own[...], one[member], two[member], three[member]), axis=0)

    q, k, v, g = (gather(own, i) for i, own in enumerate((q_ref, k_ref, v_ref, g_ref)))
    place = lax.broadcasted_iota(jnp.int32, (1, rows), 1) // TILE
    key_first = jnp.where(
        place < 2,
        jnp.where(place == 0, info[1], info[2]),
        jnp.where(place == 2, info[3], info[4]),
    )
    weights_all = []
    dscores_all = []
    for tile in range(MOST):
        part = slice(tile * TILE, (tile + 1) * TILE)
        query_rows, grad_rows = q[part], g[part]
        scores = matmul(query_rows, k, 1, 1) * factor
        scores = jnp.where(key_first == info[1 + tile], scores, -jnp.inf)
        row_max = jnp.max(scores, axis=1, keepdims=True)
        raised = jnp.exp(scores - row_max)
        weights = raised * (1.0 / jnp.sum(raised, axis=1, keepdims=True))
        half = weights.astype(jnp.bfloat16)
        attended = matmul(half, v, 1, 0).astype(jnp.bfloat16)
        delta = jnp.sum(
            grad_rows.astype(jnp.float32) * attended.astype(jnp.float32), axis=1, keepdims=True
        )
        dweights = matmul(grad_rows, v, 1, 1)
        dscores = (weights * (dweights - delta)).astype(jnp.bfloat16)
        outs[tile][0] = attended
        outs[tile][1] = (matmul(dscores, k, 1, 0) * factor).astype(jnp.bfloat16)
        weights_all.append(half)
        dscores_all.append(dscores)
    key_grad = (matmul(jnp.concatenate(dscores_all, axis=0), q, 0, 0) * factor).astype(jnp.bfloat16)
    value_grad = matmul(jnp.concatenate(weights_all, axis=0), g, 0, 0).astype(jnp.bfloat16)
    for tile in range(MOST):
        part = slice(tile * TILE, (tile + 1) * TILE)
        outs[tile][2] = key_grad[part]
        outs[tile][3] = value_grad[part]


def attend(info, arrays, received, after, begin, heads, heads_each):
    width = heads * HD
    piece = jax.ShapeDtypeStruct((4, TILE, width), jnp.bfloat16)
    own_spec = pl.BlockSpec((TILE, HD), lambda h, info: (0, info[0] * heads_each + begin + h))
    piece_spec = pl.BlockSpec((4, TILE, HD), lambda h, info: (0, 0, h))
    rows = MOST * TILE
    return pl.pallas_call(
        attend_kernel,
        out_shape=(piece,) * 4,
        grid_spec=pltpu.PrefetchScalarGridSpec(
            num_scalar_prefetch=1,
            grid=(heads,),
            in_specs=[own_spec] * 4
            + [piece_spec] * 3
            + [pl.BlockSpec(memory_space=pl.ANY)] * len(after),
            out_specs=(piece_spec,) * 4,
        ),
        compiler_params=small_grant(),
        cost_estimate=pl.CostEstimate(
            flops=12 * rows * rows * HD * heads,
            bytes_accessed=16 * rows * HD * heads,
            transcendentals=rows * rows * heads,
        ),
        name="attend",
    )(info, *arrays, *received, *after)


def shards(queries, keys, values, out_grad, tile_offset):
    arrays = (queries, keys, values, out_grad)
    columns = queries.shape[1]
    heads_each = columns // HD // MOST
    tiles = tile_offset.shape[0]
    device = lax.axis_index(AXES)
    place = (device + MOST // 2) % MOST
    firsts = jnp.arange(tiles, dtype=jnp.int32) - tile_offset

    def describe(turning):
        slots = jnp.arange(MOST)
        sources = (place - slots) % MOST if turning else place ^ slots
        return jnp.concatenate((place[None], firsts[(device - place + sources + tiles) % tiles])).astype(jnp.int32)

    infos = {turning: describe(turning) for turning in set(TURNING)}

    def exchange(pieces, turning, sign):
        return [
            lax.ppermute(piece, AXES, routes(sign * step if turning else step, tiles, turning))
            for step, piece in zip((1, 2, 3), pieces)
        ]

    begins = [sum(CHUNKS[:i]) for i in range(len(CHUNKS))]
    received, after = [], ()
    for turning, begin, heads in zip(TURNING, begins, CHUNKS):
        pieces = pack(turning, arrays, after, begin, heads, heads_each)
        after = pieces[:1]
        received.append(exchange(pieces, turning, 1))
    results, after = [], ()
    for turning, begin, heads, pieces in zip(TURNING, begins, CHUNKS, received):
        own, *others = attend(infos[turning], arrays, pieces, after, begin, heads, heads_each)
        after = (own,)
        results.append((own, *exchange(others, turning, -1)))
    held = ()
    for index, (turning, begin, heads, pieces) in enumerate(zip(TURNING, begins, CHUNKS, results)):
        for steps in [(0, 1, 2, 3)] if index < len(CHUNKS) - 1 else LAST:
            parts = [pieces[step] for step in steps]
            held = unpack(turning, steps, parts, held, begin, heads, heads_each, columns)
    return tuple(held)


def solution(mesh):
    spec = P(AXES, None)
    return jax.shard_map(
        shards,
        mesh=mesh,
        in_specs=(spec, spec, spec, spec, P()),
        out_specs=(spec, spec, spec, spec),
        check_vma=False,
    )
```

```python
from functools import partial

import jax
import jax.numpy as jnp
from jax import lax
from jax.experimental import pallas as pl
from jax.experimental.pallas import tpu as pltpu
from jax.sharding import PartitionSpec as P

HD = 128
TILE = 128
MOST = 4
AXES = ("seq", "uly")
CHUNKS = (2, 2, 2, 2, 2)
SWAPS = ((0, 3, 2, 1),) + ((0, 1, 2, 3),) * 4
LAST = [(0, 1), (2,), (3,)]


def routes(swap, tiles):
    def tile_at(window, place):
        return (MOST * window + place - MOST // 2) % tiles

    return [
        (tile_at(window, place), tile_at(window, place ^ swap))
        for window in range(tiles // MOST)
        for place in range(MOST)
    ]


def head_columns(swap, begin, heads_each, width):
    place = (lax.axis_index("uly") + MOST // 2) % MOST
    return pl.ds(pl.multiple_of(((place ^ swap) * heads_each + begin) * HD, HD), width)


def small_grant():
    return pltpu.CompilerParams(vmem_limit_bytes=16 * 1024 * 1024)


def pack_kernel(swaps, begin, heads_each, width, q_ref, k_ref, v_ref, g_ref, *rest):
    outs, sems = rest[-4:-1], rest[-1]
    copies = []
    for out, swap in enumerate(swaps[1:]):
        columns = head_columns(swap, begin, heads_each, width)
        for member, source in enumerate((q_ref, k_ref, v_ref, g_ref)):
            copies.append(
                pltpu.make_async_copy(
                    source.at[:, columns],
                    outs[out].at[member],
                    sems.at[out, member],
                )
            )
    for copy in copies:
        copy.start()
    for copy in copies:
        copy.wait()


def pack(swaps, arrays, after, begin, heads, heads_each):
    width = heads * HD
    piece = pltpu.VMEM((4, TILE, width), jnp.bfloat16)
    arrays = [pltpu.with_memory_space_constraint(array, pltpu.HBM) for array in arrays]
    return pl.pallas_call(
        partial(pack_kernel, swaps, begin, heads_each, width),
        out_shape=(piece,) * 3,
        in_specs=[pl.BlockSpec(memory_space=pl.ANY)] * (4 + len(after)),
        out_specs=(pl.BlockSpec(memory_space=pltpu.VMEM),) * 3,
        scratch_shapes=[pltpu.SemaphoreType.DMA((3, 4))],
        compiler_params=small_grant(),
        cost_estimate=pl.CostEstimate(flops=0, bytes_accessed=24 * TILE * width * 2, transcendentals=0),
        name="pack",
    )(*arrays, *after)


def unpack_kernel(swaps, begin, heads_each, width, *rest):
    pieces = rest[: len(swaps)]
    outs, sems = rest[-5:-1], rest[-1]
    copies = []
    for index, swap in enumerate(swaps):
        columns = head_columns(swap, begin, heads_each, width)
        for member, target in enumerate(outs):
            copies.append(
                pltpu.make_async_copy(
                    pieces[index].at[member],
                    target.at[:, columns],
                    sems.at[index, member],
                )
            )
    for copy in copies:
        copy.start()
    for copy in copies:
        copy.wait()


def unpack(swaps, pieces, held, begin, heads, heads_each, columns):
    width = heads * HD
    whole = jax.ShapeDtypeStruct((TILE, columns), jnp.bfloat16)
    return pl.pallas_call(
        partial(unpack_kernel, swaps, begin, heads_each, width),
        out_shape=(whole,) * 4,
        in_specs=[pl.BlockSpec(memory_space=pltpu.VMEM)] * len(swaps)
        + [pl.BlockSpec(memory_space=pl.ANY)] * len(held),
        out_specs=(pl.BlockSpec(memory_space=pl.ANY),) * 4,
        scratch_shapes=[pltpu.SemaphoreType.DMA((len(swaps), 4))],
        compiler_params=small_grant(),
        input_output_aliases={len(swaps) + i: i for i in range(len(held))},
        cost_estimate=pl.CostEstimate(flops=0, bytes_accessed=8 * len(swaps) * TILE * width * 2, transcendentals=0),
        name="unpack",
    )(*pieces, *held)


def matmul(left, right, left_dim, right_dim):
    return lax.dot_general(
        left, right, (((left_dim,), (right_dim,)), ((), ())), preferred_element_type=jnp.float32
    )


def attend_kernel(info, q_ref, k_ref, v_ref, g_ref, one, two, three, *rest):
    outs = rest[-4:]
    factor = HD ** -0.5
    rows = MOST * TILE

    def gather(own, member):
        return jnp.concatenate((own[...], one[member], two[member], three[member]), axis=0)

    q, k, v, g = (gather(own, i) for i, own in enumerate((q_ref, k_ref, v_ref, g_ref)))
    place = lax.broadcasted_iota(jnp.int32, (1, rows), 1) // TILE
    key_first = jnp.where(
        place < 2,
        jnp.where(place == 0, info[1], info[2]),
        jnp.where(place == 2, info[3], info[4]),
    )
    weights_all = []
    dscores_all = []
    for tile in range(MOST):
        part = slice(tile * TILE, (tile + 1) * TILE)
        query_rows, grad_rows = q[part], g[part]
        scores = matmul(query_rows, k, 1, 1) * factor
        scores = jnp.where(key_first == info[1 + tile], scores, -jnp.inf)
        row_max = jnp.max(scores, axis=1, keepdims=True)
        raised = jnp.exp(scores - row_max)
        weights = raised * (1.0 / jnp.sum(raised, axis=1, keepdims=True))
        half = weights.astype(jnp.bfloat16)
        attended = matmul(half, v, 1, 0).astype(jnp.bfloat16)
        delta = jnp.sum(
            grad_rows.astype(jnp.float32) * attended.astype(jnp.float32), axis=1, keepdims=True
        )
        dweights = matmul(grad_rows, v, 1, 1)
        dscores = (weights * (dweights - delta)).astype(jnp.bfloat16)
        outs[tile][0] = attended
        outs[tile][1] = (matmul(dscores, k, 1, 0) * factor).astype(jnp.bfloat16)
        weights_all.append(half)
        dscores_all.append(dscores)
    key_grad = (matmul(jnp.concatenate(dscores_all, axis=0), q, 0, 0) * factor).astype(jnp.bfloat16)
    value_grad = matmul(jnp.concatenate(weights_all, axis=0), g, 0, 0).astype(jnp.bfloat16)
    for tile in range(MOST):
        part = slice(tile * TILE, (tile + 1) * TILE)
        outs[tile][2] = key_grad[part]
        outs[tile][3] = value_grad[part]


def attend(info, arrays, received, after, begin, heads, heads_each):
    width = heads * HD
    piece = jax.ShapeDtypeStruct((4, TILE, width), jnp.bfloat16)
    own_spec = pl.BlockSpec((TILE, HD), lambda h, info: (0, info[0] * heads_each + begin + h))
    piece_spec = pl.BlockSpec((4, TILE, HD), lambda h, info: (0, 0, h))
    rows = MOST * TILE
    return pl.pallas_call(
        attend_kernel,
        out_shape=(piece,) * 4,
        grid_spec=pltpu.PrefetchScalarGridSpec(
            num_scalar_prefetch=1,
            grid=(heads,),
            in_specs=[own_spec] * 4
            + [piece_spec] * 3
            + [pl.BlockSpec(memory_space=pl.ANY)] * len(after),
            out_specs=(piece_spec,) * 4,
        ),
        compiler_params=small_grant(),
        cost_estimate=pl.CostEstimate(
            flops=12 * rows * rows * HD * heads,
            bytes_accessed=16 * rows * HD * heads,
            transcendentals=rows * rows * heads,
        ),
        name="attend",
    )(info, *arrays, *received, *after)


def shards(queries, keys, values, out_grad, tile_offset):
    arrays = (queries, keys, values, out_grad)
    columns = queries.shape[1]
    heads_each = columns // HD // MOST
    tiles = tile_offset.shape[0]
    device = lax.axis_index(AXES)
    place = (device + MOST // 2) % MOST
    firsts = jnp.arange(tiles, dtype=jnp.int32) - tile_offset

    def describe(swaps):
        sources = place ^ jnp.array(swaps)
        return jnp.concatenate((place[None], firsts[(device - place + sources + tiles) % tiles])).astype(jnp.int32)

    infos = {swaps: describe(swaps) for swaps in dict.fromkeys(SWAPS)}

    def exchange(pieces, swaps):
        return [lax.ppermute(piece, AXES, routes(swap, tiles)) for swap, piece in zip(swaps[1:], pieces)]

    begins = [sum(CHUNKS[:i]) for i in range(len(CHUNKS))]
    received, after = [], ()
    for swaps, begin, heads in zip(SWAPS, begins, CHUNKS):
        pieces = pack(swaps, arrays, after, begin, heads, heads_each)
        after = pieces[:1]
        received.append(exchange(pieces, swaps))
    results, after = [], ()
    for swaps, begin, heads, pieces in zip(SWAPS, begins, CHUNKS, received):
        own, *others = attend(infos[swaps], arrays, pieces, after, begin, heads, heads_each)
        after = (own,)
        results.append((own, *exchange(others, swaps)))
    held = ()
    for index, (swaps, begin, heads, pieces) in enumerate(zip(SWAPS, begins, CHUNKS, results)):
        for steps in [(0, 1, 2, 3)] if index < len(CHUNKS) - 1 else LAST:
            parts, to = [pieces[step] for step in steps], [swaps[step] for step in steps]
            held = unpack(to, parts, held, begin, heads, heads_each, columns)
    return tuple(held)


def solution(mesh):
    spec = P(AXES, None)
    return jax.shard_map(
        shards,
        mesh=mesh,
        in_specs=(spec, spec, spec, spec, P()),
        out_specs=(spec, spec, spec, spec),
        check_vma=False,
    )
```

```python
from functools import partial

import jax
import jax.numpy as jnp
from jax import lax
from jax.experimental import pallas as pl
from jax.experimental.pallas import tpu as pltpu
from jax.sharding import PartitionSpec as P

HD = 128
TILE = 128
MOST = 4
AXES = ("seq", "uly")
CHUNKS = (2, 2, 2, 2, 2)
SWAPS = ((0, 3, 2, 1),) + ((0, 2, 1, 3),) * 4
LAST = [(0, 1), (2,), (3,)]


def routes(swap, tiles):
    def tile_at(window, place):
        return (MOST * window + place - MOST // 2) % tiles

    return [
        (tile_at(window, place), tile_at(window, place ^ swap))
        for window in range(tiles // MOST)
        for place in range(MOST)
    ]


def head_columns(swap, begin, heads_each, width):
    place = (lax.axis_index("uly") + MOST // 2) % MOST
    return pl.ds(pl.multiple_of(((place ^ swap) * heads_each + begin) * HD, HD), width)


def small_grant():
    return pltpu.CompilerParams(vmem_limit_bytes=16 * 1024 * 1024)


def pack_kernel(swaps, begin, heads_each, width, q_ref, k_ref, v_ref, g_ref, *rest):
    outs, sems = rest[-4:-1], rest[-1]
    copies = []
    for out, swap in enumerate(swaps[1:]):
        columns = head_columns(swap, begin, heads_each, width)
        for member, source in enumerate((q_ref, k_ref, v_ref, g_ref)):
            copies.append(
                pltpu.make_async_copy(
                    source.at[:, columns],
                    outs[out].at[member],
                    sems.at[out, member],
                )
            )
    for copy in copies:
        copy.start()
    for copy in copies:
        copy.wait()


def pack(swaps, arrays, after, begin, heads, heads_each):
    width = heads * HD
    piece = pltpu.VMEM((4, TILE, width), jnp.bfloat16)
    arrays = [pltpu.with_memory_space_constraint(array, pltpu.HBM) for array in arrays]
    return pl.pallas_call(
        partial(pack_kernel, swaps, begin, heads_each, width),
        out_shape=(piece,) * 3,
        in_specs=[pl.BlockSpec(memory_space=pl.ANY)] * (4 + len(after)),
        out_specs=(pl.BlockSpec(memory_space=pltpu.VMEM),) * 3,
        scratch_shapes=[pltpu.SemaphoreType.DMA((3, 4))],
        compiler_params=small_grant(),
        cost_estimate=pl.CostEstimate(flops=0, bytes_accessed=24 * TILE * width * 2, transcendentals=0),
        name="pack",
    )(*arrays, *after)


def unpack_kernel(swaps, begin, heads_each, width, *rest):
    pieces = rest[: len(swaps)]
    outs, sems = rest[-5:-1], rest[-1]
    copies = []
    for index, swap in enumerate(swaps):
        columns = head_columns(swap, begin, heads_each, width)
        for member, target in enumerate(outs):
            copies.append(
                pltpu.make_async_copy(
                    pieces[index].at[member],
                    target.at[:, columns],
                    sems.at[index, member],
                )
            )
    for copy in copies:
        copy.start()
    for copy in copies:
        copy.wait()


def unpack(swaps, pieces, held, begin, heads, heads_each, columns):
    width = heads * HD
    whole = jax.ShapeDtypeStruct((TILE, columns), jnp.bfloat16)
    return pl.pallas_call(
        partial(unpack_kernel, swaps, begin, heads_each, width),
        out_shape=(whole,) * 4,
        in_specs=[pl.BlockSpec(memory_space=pltpu.VMEM)] * len(swaps)
        + [pl.BlockSpec(memory_space=pl.ANY)] * len(held),
        out_specs=(pl.BlockSpec(memory_space=pl.ANY),) * 4,
        scratch_shapes=[pltpu.SemaphoreType.DMA((len(swaps), 4))],
        compiler_params=small_grant(),
        input_output_aliases={len(swaps) + i: i for i in range(len(held))},
        cost_estimate=pl.CostEstimate(flops=0, bytes_accessed=8 * len(swaps) * TILE * width * 2, transcendentals=0),
        name="unpack",
    )(*pieces, *held)


def matmul(left, right, left_dim, right_dim):
    return lax.dot_general(
        left, right, (((left_dim,), (right_dim,)), ((), ())), preferred_element_type=jnp.float32
    )


def attend_kernel(info, q_ref, k_ref, v_ref, g_ref, one, two, three, *rest):
    outs = rest[-4:]
    factor = HD ** -0.5
    rows = MOST * TILE

    def gather(own, member):
        return jnp.concatenate((own[...], one[member], two[member], three[member]), axis=0)

    q, k, v, g = (gather(own, i) for i, own in enumerate((q_ref, k_ref, v_ref, g_ref)))
    place = lax.broadcasted_iota(jnp.int32, (1, rows), 1) // TILE
    key_first = jnp.where(
        place < 2,
        jnp.where(place == 0, info[1], info[2]),
        jnp.where(place == 2, info[3], info[4]),
    )
    weights_all = []
    dscores_all = []
    for tile in range(MOST):
        part = slice(tile * TILE, (tile + 1) * TILE)
        query_rows, grad_rows = q[part], g[part]
        scores = matmul(query_rows, k, 1, 1) * factor
        scores = jnp.where(key_first == info[1 + tile], scores, -jnp.inf)
        row_max = jnp.max(scores, axis=1, keepdims=True)
        raised = jnp.exp(scores - row_max)
        weights = raised * (1.0 / jnp.sum(raised, axis=1, keepdims=True))
        half = weights.astype(jnp.bfloat16)
        attended = matmul(half, v, 1, 0).astype(jnp.bfloat16)
        delta = jnp.sum(
            grad_rows.astype(jnp.float32) * attended.astype(jnp.float32), axis=1, keepdims=True
        )
        dweights = matmul(grad_rows, v, 1, 1)
        dscores = (weights * (dweights - delta)).astype(jnp.bfloat16)
        outs[tile][0] = attended
        outs[tile][1] = (matmul(dscores, k, 1, 0) * factor).astype(jnp.bfloat16)
        weights_all.append(half)
        dscores_all.append(dscores)
    key_grad = (matmul(jnp.concatenate(dscores_all, axis=0), q, 0, 0) * factor).astype(jnp.bfloat16)
    value_grad = matmul(jnp.concatenate(weights_all, axis=0), g, 0, 0).astype(jnp.bfloat16)
    for tile in range(MOST):
        part = slice(tile * TILE, (tile + 1) * TILE)
        outs[tile][2] = key_grad[part]
        outs[tile][3] = value_grad[part]


def attend(info, arrays, received, after, begin, heads, heads_each):
    width = heads * HD
    piece = jax.ShapeDtypeStruct((4, TILE, width), jnp.bfloat16)
    own_spec = pl.BlockSpec((TILE, HD), lambda h, info: (0, info[0] * heads_each + begin + h))
    piece_spec = pl.BlockSpec((4, TILE, HD), lambda h, info: (0, 0, h))
    rows = MOST * TILE
    return pl.pallas_call(
        attend_kernel,
        out_shape=(piece,) * 4,
        grid_spec=pltpu.PrefetchScalarGridSpec(
            num_scalar_prefetch=1,
            grid=(heads,),
            in_specs=[own_spec] * 4
            + [piece_spec] * 3
            + [pl.BlockSpec(memory_space=pl.ANY)] * len(after),
            out_specs=(piece_spec,) * 4,
        ),
        compiler_params=small_grant(),
        cost_estimate=pl.CostEstimate(
            flops=12 * rows * rows * HD * heads,
            bytes_accessed=16 * rows * HD * heads,
            transcendentals=rows * rows * heads,
        ),
        name="attend",
    )(info, *arrays, *received, *after)


def shards(queries, keys, values, out_grad, tile_offset):
    arrays = (queries, keys, values, out_grad)
    columns = queries.shape[1]
    heads_each = columns // HD // MOST
    tiles = tile_offset.shape[0]
    device = lax.axis_index(AXES)
    place = (device + MOST // 2) % MOST
    firsts = jnp.arange(tiles, dtype=jnp.int32) - tile_offset

    def describe(swaps):
        sources = place ^ jnp.array(swaps)
        return jnp.concatenate((place[None], firsts[(device - place + sources + tiles) % tiles])).astype(jnp.int32)

    infos = {swaps: describe(swaps) for swaps in dict.fromkeys(SWAPS)}

    def exchange(pieces, swaps):
        return [lax.ppermute(piece, AXES, routes(swap, tiles)) for swap, piece in zip(swaps[1:], pieces)]

    begins = [sum(CHUNKS[:i]) for i in range(len(CHUNKS))]
    received, after = [], ()
    for swaps, begin, heads in zip(SWAPS, begins, CHUNKS):
        pieces = pack(swaps, arrays, after, begin, heads, heads_each)
        after = pieces[:1]
        received.append(exchange(pieces, swaps))
    results, after = [], ()
    for swaps, begin, heads, pieces in zip(SWAPS, begins, CHUNKS, received):
        own, *others = attend(infos[swaps], arrays, pieces, after, begin, heads, heads_each)
        after = (own,)
        results.append((own, *exchange(others, swaps)))
    held = ()
    for index, (swaps, begin, heads, pieces) in enumerate(zip(SWAPS, begins, CHUNKS, results)):
        for steps in [(0, 1, 2, 3)] if index < len(CHUNKS) - 1 else LAST:
            parts, to = [pieces[step] for step in steps], [swaps[step] for step in steps]
            held = unpack(to, parts, held, begin, heads, heads_each, columns)
    return tuple(held)


def solution(mesh):
    spec = P(AXES, None)
    return jax.shard_map(
        shards,
        mesh=mesh,
        in_specs=(spec, spec, spec, spec, P()),
        out_specs=(spec, spec, spec, spec),
        check_vma=False,
    )
```

```python
from functools import partial

import jax
import jax.numpy as jnp
from jax import lax
from jax.experimental import pallas as pl
from jax.experimental.pallas import tpu as pltpu
from jax.sharding import PartitionSpec as P

HD = 128
TILE = 128
MOST = 4
AXES = ("seq", "uly")
CHUNKS = (2, 2, 2, 2, 2)
SWAPS = ((0, 3, 2, 1),) + ((0, 2, 3, 1),) * 4
LAST = [(0, 1), (2,), (3,)]


def routes(swap, tiles):
    def tile_at(window, place):
        return (MOST * window + place - MOST // 2) % tiles

    return [
        (tile_at(window, place), tile_at(window, place ^ swap))
        for window in range(tiles // MOST)
        for place in range(MOST)
    ]


def head_columns(swap, begin, heads_each, width):
    place = (lax.axis_index("uly") + MOST // 2) % MOST
    return pl.ds(pl.multiple_of(((place ^ swap) * heads_each + begin) * HD, HD), width)


def small_grant():
    return pltpu.CompilerParams(vmem_limit_bytes=16 * 1024 * 1024)


def pack_kernel(swaps, begin, heads_each, width, q_ref, k_ref, v_ref, g_ref, *rest):
    outs, sems = rest[-4:-1], rest[-1]
    copies = []
    for out, swap in enumerate(swaps[1:]):
        columns = head_columns(swap, begin, heads_each, width)
        for member, source in enumerate((q_ref, k_ref, v_ref, g_ref)):
            copies.append(
                pltpu.make_async_copy(
                    source.at[:, columns],
                    outs[out].at[member],
                    sems.at[out, member],
                )
            )
    for copy in copies:
        copy.start()
    for copy in copies:
        copy.wait()


def pack(swaps, arrays, after, begin, heads, heads_each):
    width = heads * HD
    piece = pltpu.VMEM((4, TILE, width), jnp.bfloat16)
    arrays = [pltpu.with_memory_space_constraint(array, pltpu.HBM) for array in arrays]
    return pl.pallas_call(
        partial(pack_kernel, swaps, begin, heads_each, width),
        out_shape=(piece,) * 3,
        in_specs=[pl.BlockSpec(memory_space=pl.ANY)] * (4 + len(after)),
        out_specs=(pl.BlockSpec(memory_space=pltpu.VMEM),) * 3,
        scratch_shapes=[pltpu.SemaphoreType.DMA((3, 4))],
        compiler_params=small_grant(),
        cost_estimate=pl.CostEstimate(flops=0, bytes_accessed=24 * TILE * width * 2, transcendentals=0),
        name="pack",
    )(*arrays, *after)


def unpack_kernel(swaps, begin, heads_each, width, *rest):
    pieces = rest[: len(swaps)]
    outs, sems = rest[-5:-1], rest[-1]
    copies = []
    for index, swap in enumerate(swaps):
        columns = head_columns(swap, begin, heads_each, width)
        for member, target in enumerate(outs):
            copies.append(
                pltpu.make_async_copy(
                    pieces[index].at[member],
                    target.at[:, columns],
                    sems.at[index, member],
                )
            )
    for copy in copies:
        copy.start()
    for copy in copies:
        copy.wait()


def unpack(swaps, pieces, held, begin, heads, heads_each, columns):
    width = heads * HD
    whole = jax.ShapeDtypeStruct((TILE, columns), jnp.bfloat16)
    return pl.pallas_call(
        partial(unpack_kernel, swaps, begin, heads_each, width),
        out_shape=(whole,) * 4,
        in_specs=[pl.BlockSpec(memory_space=pltpu.VMEM)] * len(swaps)
        + [pl.BlockSpec(memory_space=pl.ANY)] * len(held),
        out_specs=(pl.BlockSpec(memory_space=pl.ANY),) * 4,
        scratch_shapes=[pltpu.SemaphoreType.DMA((len(swaps), 4))],
        compiler_params=small_grant(),
        input_output_aliases={len(swaps) + i: i for i in range(len(held))},
        cost_estimate=pl.CostEstimate(flops=0, bytes_accessed=8 * len(swaps) * TILE * width * 2, transcendentals=0),
        name="unpack",
    )(*pieces, *held)


def matmul(left, right, left_dim, right_dim):
    return lax.dot_general(
        left, right, (((left_dim,), (right_dim,)), ((), ())), preferred_element_type=jnp.float32
    )


def attend_kernel(info, q_ref, k_ref, v_ref, g_ref, one, two, three, *rest):
    outs = rest[-4:]
    factor = HD ** -0.5
    rows = MOST * TILE

    def gather(own, member):
        return jnp.concatenate((own[...], one[member], two[member], three[member]), axis=0)

    q, k, v, g = (gather(own, i) for i, own in enumerate((q_ref, k_ref, v_ref, g_ref)))
    place = lax.broadcasted_iota(jnp.int32, (1, rows), 1) // TILE
    key_first = jnp.where(
        place < 2,
        jnp.where(place == 0, info[1], info[2]),
        jnp.where(place == 2, info[3], info[4]),
    )
    weights_all = []
    dscores_all = []
    for tile in range(MOST):
        part = slice(tile * TILE, (tile + 1) * TILE)
        query_rows, grad_rows = q[part], g[part]
        scores = matmul(query_rows, k, 1, 1) * factor
        scores = jnp.where(key_first == info[1 + tile], scores, -jnp.inf)
        row_max = jnp.max(scores, axis=1, keepdims=True)
        raised = jnp.exp(scores - row_max)
        weights = raised * (1.0 / jnp.sum(raised, axis=1, keepdims=True))
        half = weights.astype(jnp.bfloat16)
        attended = matmul(half, v, 1, 0).astype(jnp.bfloat16)
        delta = jnp.sum(
            grad_rows.astype(jnp.float32) * attended.astype(jnp.float32), axis=1, keepdims=True
        )
        dweights = matmul(grad_rows, v, 1, 1)
        dscores = (weights * (dweights - delta)).astype(jnp.bfloat16)
        outs[tile][0] = attended
        outs[tile][1] = (matmul(dscores, k, 1, 0) * factor).astype(jnp.bfloat16)
        weights_all.append(half)
        dscores_all.append(dscores)
    key_grad = (matmul(jnp.concatenate(dscores_all, axis=0), q, 0, 0) * factor).astype(jnp.bfloat16)
    value_grad = matmul(jnp.concatenate(weights_all, axis=0), g, 0, 0).astype(jnp.bfloat16)
    for tile in range(MOST):
        part = slice(tile * TILE, (tile + 1) * TILE)
        outs[tile][2] = key_grad[part]
        outs[tile][3] = value_grad[part]


def attend(info, arrays, received, after, begin, heads, heads_each):
    width = heads * HD
    piece = jax.ShapeDtypeStruct((4, TILE, width), jnp.bfloat16)
    own_spec = pl.BlockSpec((TILE, HD), lambda h, info: (0, info[0] * heads_each + begin + h))
    piece_spec = pl.BlockSpec((4, TILE, HD), lambda h, info: (0, 0, h))
    rows = MOST * TILE
    return pl.pallas_call(
        attend_kernel,
        out_shape=(piece,) * 4,
        grid_spec=pltpu.PrefetchScalarGridSpec(
            num_scalar_prefetch=1,
            grid=(heads,),
            in_specs=[own_spec] * 4
            + [piece_spec] * 3
            + [pl.BlockSpec(memory_space=pl.ANY)] * len(after),
            out_specs=(piece_spec,) * 4,
        ),
        compiler_params=small_grant(),
        cost_estimate=pl.CostEstimate(
            flops=12 * rows * rows * HD * heads,
            bytes_accessed=16 * rows * HD * heads,
            transcendentals=rows * rows * heads,
        ),
        name="attend",
    )(info, *arrays, *received, *after)


def shards(queries, keys, values, out_grad, tile_offset):
    arrays = (queries, keys, values, out_grad)
    columns = queries.shape[1]
    heads_each = columns // HD // MOST
    tiles = tile_offset.shape[0]
    device = lax.axis_index(AXES)
    place = (device + MOST // 2) % MOST
    firsts = jnp.arange(tiles, dtype=jnp.int32) - tile_offset

    def describe(swaps):
        sources = place ^ jnp.array(swaps)
        return jnp.concatenate((place[None], firsts[(device - place + sources + tiles) % tiles])).astype(jnp.int32)

    infos = {swaps: describe(swaps) for swaps in dict.fromkeys(SWAPS)}

    def exchange(pieces, swaps):
        return [lax.ppermute(piece, AXES, routes(swap, tiles)) for swap, piece in zip(swaps[1:], pieces)]

    begins = [sum(CHUNKS[:i]) for i in range(len(CHUNKS))]
    received, after = [], ()
    for swaps, begin, heads in zip(SWAPS, begins, CHUNKS):
        pieces = pack(swaps, arrays, after, begin, heads, heads_each)
        after = pieces[:1]
        received.append(exchange(pieces, swaps))
    results, after = [], ()
    for swaps, begin, heads, pieces in zip(SWAPS, begins, CHUNKS, received):
        own, *others = attend(infos[swaps], arrays, pieces, after, begin, heads, heads_each)
        after = (own,)
        results.append((own, *exchange(others, swaps)))
    held = ()
    for index, (swaps, begin, heads, pieces) in enumerate(zip(SWAPS, begins, CHUNKS, results)):
        for steps in [(0, 1, 2, 3)] if index < len(CHUNKS) - 1 else LAST:
            parts, to = [pieces[step] for step in steps], [swaps[step] for step in steps]
            held = unpack(to, parts, held, begin, heads, heads_each, columns)
    return tuple(held)


def solution(mesh):
    spec = P(AXES, None)
    return jax.shard_map(
        shards,
        mesh=mesh,
        in_specs=(spec, spec, spec, spec, P()),
        out_specs=(spec, spec, spec, spec),
        check_vma=False,
    )
```
